32 devices in a mesh: ctx: 16 (over z, y, core), head: 2 (over x).
Axes of the slice: x: 2, y: 2, z: 4, core: 2. Of those that a mesh axis runs over, the one named last changes fastest.
Arguments:
- features: bfloat16 [8192, 5376], P('ctx', 'head'), may hold values from -30 to 30
- query_weight: bfloat16 [5376, 4096], P('ctx', 'head'), as said below
- key_weight: bfloat16 [5376, 2048], P('ctx', 'head'), as said below
- value_weight: bfloat16 [5376, 2048], P('ctx', 'head'), may hold values from -0.078125 to 0.078125
- doc_lengths: int32 [4], replicated, may hold values from 1 to 4096, 8192 in all
- out_grad: bfloat16 [8192, 4096], P('ctx', 'head'), may hold values from -6 to 6
Outputs:
- attention: bfloat16 [8192, 4096], P('ctx', 'head')
- key_weight_grad: bfloat16 [5376, 2048], P('ctx', 'head')
- value_weight_grad: bfloat16 [5376, 2048], P('ctx', 'head')
The draws below stay inside these ranges and needn't reach their ends.
Inputs may be any that keep to these rules, and one draw needn't show every extreme that they name: `doc_lengths`: the lengths sum to 8192; the longest document holds half of them. `query_weight`: projection entries. `key_weight`: projection entries.
All inputs are finite; a program needn't handle non-finite values.
Results may differ from the reference program's by a relative error of at most 0.029.
Values may be sent and summed in bfloat16 or wider, within the bound.
A program may use at most 192 MiB of HBM per device.

```python
import math
import jax
import jax.numpy as jnp
import numpy as np
from jax import lax

D = 5376
HEADS_Q = 32
HEADS_KV = 16
HEAD_DIM = 128
WINDOW = 1024
TOK_DEV = 512
SPAN = 2
TOKENS = 8192
DOCS = 4
N_CTX = 16


def query_base(key):
    raw = jnp.clip(jax.random.normal(jax.random.fold_in(key, 11), (D, HEADS_Q * HEAD_DIM), jnp.float32), -6.0, 6.0)
    return raw / jnp.sqrt(jnp.float32(D))


def draw_query_weight(key, part):
    return query_base(key).astype(jnp.bfloat16)


def draw_key_weight(key, part):
    noise = jnp.clip(jax.random.normal(jax.random.fold_in(key, 12), (D, HEADS_KV * HEAD_DIM), jnp.float32), -6.0, 6.0) / jnp.sqrt(jnp.float32(D))
    return noise.astype(jnp.bfloat16)


def draw_features(key, part):
    return jnp.clip(jax.random.normal(jax.random.fold_in(key, 1), (TOKENS, D), jnp.float32), -6.0, 6.0).astype(jnp.bfloat16)


def shard_levels(own_key, extent, cuts, low, top_value):
    gain = 1.0
    for axis_at, blocks in cuts:
        heights = jax.random.uniform(jax.random.fold_in(jax.random.fold_in(own_key, 6), axis_at), (blocks,), jnp.float32, low / len(cuts), top_value / len(cuts))
        gain = gain * jnp.repeat(jnp.exp(heights), extent[axis_at] // blocks).reshape((-1,) + (1,) * (len(extent) - 1 - axis_at))
    return gain


def profile(number_of, total, reach, skew):
    loads = [(1 << 20) // math.isqrt(standing ** skew) + 1 for standing in range(2, number_of + 1)]
    surplus, given = total - reach - (number_of - 1), [1] * (number_of - 1)
    while surplus > 0:
        free = [i for i in range(number_of - 1) if given[i] < reach]
        mass, remaining = sum([loads[i] for i in free]), surplus
        for i in free:
            more = min(reach - given[i], max(1, remaining * loads[i] // mass), surplus)
            given[i] = given[i] + more
            surplus = surplus - more
    return np.array([reach] + given)


def uneven_parts(key, amount, total, bound, skew):
    if amount == 2:
        one = jax.random.randint(key, (), max(1, total - bound), min(bound, total - 1) + 1)
        return jnp.stack([one, total - one])
    tallies = jnp.asarray(profile(amount, total, bound, skew), jnp.int32)
    couples = (amount - 1) // 2
    source_of, receiver = tallies[1:1 + 2 * couples:2], tallies[2:2 + 2 * couples:2]
    slack = jnp.minimum(source_of - 1, bound - receiver)
    passed = jax.random.randint(jax.random.fold_in(key, 1), (couples,), 0, 1 << 20) % (slack + 1)
    tallies = tallies.at[1:1 + 2 * couples:2].set(source_of - passed).at[2:2 + 2 * couples:2].set(receiver + passed)
    return tallies[jax.random.permutation(jax.random.fold_in(key, 2), amount)]


def normal_values(rng, dims, spread, most, split=(), kind=jnp.bfloat16):
    values = spread * jax.random.normal(rng, dims, jnp.float32)
    if split:
        values = values * shard_levels(rng, dims, split, -0.22, 0.18)
    return jnp.clip(values, -most, most).astype(kind)


def setup_inputs(seed: int = 0) -> dict:
    splits = jax.random.split(jax.random.key(seed), 7)
    return {
        "features": draw_features(jax.random.fold_in(splits[6], 71), 0),
        "query_weight": draw_query_weight(jax.random.fold_in(splits[6], 71), 0),
        "key_weight": draw_key_weight(jax.random.fold_in(splits[6], 71), 0),
        "value_weight": normal_values(splits[3], (D, HEADS_KV * HEAD_DIM), D ** -0.5, 0.078125, ((0, 16), (1, 2))),
        "doc_lengths": uneven_parts(splits[4], DOCS, TOKENS, TOKENS // 2, 2).astype(jnp.int32),
        "out_grad": normal_values(splits[5], (TOKENS, HEADS_Q * HEAD_DIM), 1.0, 6.0, ((0, 16), (1, 2))),
    }


ROPE_BASE = 10000.0


def rotate_half(values):
    middle = values.shape[-1] // 2
    return jnp.concatenate([-values[..., middle:], values[..., :middle]], axis=-1)


def rope_tables(offsets):
    middle = HEAD_DIM // 2
    inverse = ROPE_BASE ** (-(jnp.arange(middle).astype(jnp.float32) * 2.0 / HEAD_DIM))
    angles = offsets.astype(jnp.float32)[:, None] * inverse[None, :]
    cosine = jnp.cos(angles)
    sine_table = jnp.sin(angles)
    return jnp.concatenate([cosine, cosine], axis=-1), jnp.concatenate([sine_table, sine_table], axis=-1)


def rotate(values, cosine, sine_table):
    return values * cosine[:, None, :] + rotate_half(values) * sine_table[:, None, :]


def unrotate(values, cosine, sine_table):
    return values * cosine[:, None, :] - rotate_half(values) * sine_table[:, None, :]


def start_of(positions, starts):
    candidates = jnp.where(starts[None, :] <= positions[:, None], starts[None, :], -1)
    return jnp.max(candidates, axis=1).astype(jnp.int32)


def rounded(values):
    return lax.optimization_barrier(values.astype(jnp.bfloat16)).astype(jnp.float32)


def reference(features, query_weight, key_weight, value_weight, doc_lengths, out_grad):
    highest = lax.Precision.HIGHEST
    query_scale = (D / HEADS_Q) ** -0.5
    group_size = HEADS_Q // HEADS_KV
    starts = (jnp.cumsum(doc_lengths) - doc_lengths).astype(jnp.int32)
    token_index = jnp.arange(TOKENS, dtype=jnp.int32)
    token_start = start_of(token_index, starts)
    cosine, sine_table = rope_tables(token_index - token_start)
    query_proj = jnp.dot(features, query_weight, preferred_element_type=jnp.float32).reshape(TOKENS, HEADS_Q, HEAD_DIM)
    key_proj = jnp.dot(features, key_weight, preferred_element_type=jnp.float32).reshape(TOKENS, HEADS_KV, HEAD_DIM)
    value_proj = jnp.dot(features, value_weight, preferred_element_type=jnp.float32).reshape(TOKENS, HEADS_KV, HEAD_DIM)
    queries = (rotate(query_proj, cosine, sine_table) * query_scale).astype(jnp.bfloat16)
    keys_all = rotate(key_proj, cosine, sine_table).astype(jnp.bfloat16)
    values_all = value_proj.astype(jnp.bfloat16)
    pad_rows = SPAN * TOK_DEV
    key_rows = (SPAN + 1) * TOK_DEV
    zero_rows = jnp.zeros((pad_rows, HEADS_KV, HEAD_DIM), jnp.bfloat16)
    keys_pad = jnp.concatenate([zero_rows, keys_all], axis=0)
    values_pad = jnp.concatenate([zero_rows, values_all], axis=0)
    start_pad = jnp.concatenate([jnp.full((pad_rows,), -1, jnp.int32), token_start], axis=0)
    grouped_all = queries.reshape(TOKENS, HEADS_KV, group_size, HEAD_DIM)
    grads_all = out_grad.reshape(TOKENS, HEADS_KV, group_size, HEAD_DIM)

    def block_step(running, block_index):
        key_acc, value_acc = running
        first_row = (block_index * TOK_DEV).astype(jnp.int32)
        grouped = lax.dynamic_slice_in_dim(grouped_all, first_row, TOK_DEV, 0)
        grad_heads = lax.dynamic_slice_in_dim(grads_all, first_row, TOK_DEV, 0)
        key_block = lax.dynamic_slice_in_dim(keys_pad, first_row, key_rows, 0)
        value_block = lax.dynamic_slice_in_dim(values_pad, first_row, key_rows, 0)
        query_start = lax.dynamic_slice_in_dim(token_start, first_row, TOK_DEV, 0)
        key_start = lax.dynamic_slice_in_dim(start_pad, first_row, key_rows, 0)
        query_index = first_row + jnp.arange(TOK_DEV, dtype=jnp.int32)
        key_index = first_row - pad_rows + jnp.arange(key_rows, dtype=jnp.int32)
        offsets_qk = query_index[:, None] - key_index[None, :]
        allowed = (key_index[None, :] >= 0) & (offsets_qk >= 0) & (offsets_qk < WINDOW) & (query_start[:, None] == key_start[None, :])
        scores = jnp.einsum("tkgd,skd->kgts", grouped.astype(jnp.float32), key_block.astype(jnp.float32), precision=highest)
        row_max = jnp.max(jnp.where(allowed, scores, -jnp.inf), axis=-1, keepdims=True)
        raw_weights = jnp.where(allowed, jnp.exp(scores - row_max), 0.0)
        prob_soft = raw_weights / jnp.sum(raw_weights, axis=-1, keepdims=True)
        probs_low = prob_soft.astype(jnp.bfloat16)
        attended = jnp.einsum("kgts,skd->tkgd", probs_low.astype(jnp.float32), value_block.astype(jnp.float32), precision=highest).astype(jnp.bfloat16)
        out_dot = jnp.einsum("tkgd,tkgd->kgt", grad_heads.astype(jnp.float32), attended.astype(jnp.float32), precision=highest)[..., None]
        value_partial = jnp.einsum("kgts,tkgd->skd", probs_low.astype(jnp.float32), grad_heads.astype(jnp.float32), precision=highest)
        prob_grad = jnp.einsum("tkgd,skd->kgts", grad_heads.astype(jnp.float32), value_block.astype(jnp.float32), precision=highest)
        score_grad = (prob_soft * (prob_grad - out_dot)).astype(jnp.bfloat16)
        key_partial = jnp.einsum("kgts,tkgd->skd", score_grad.astype(jnp.float32), grouped.astype(jnp.float32), precision=highest)
        key_acc = lax.dynamic_update_slice_in_dim(key_acc, lax.dynamic_slice_in_dim(key_acc, first_row, key_rows, 0) + key_partial, first_row, 0)
        value_acc = lax.dynamic_update_slice_in_dim(value_acc, lax.dynamic_slice_in_dim(value_acc, first_row, key_rows, 0) + value_partial, first_row, 0)
        return (key_acc, value_acc), attended

    empty_acc = jnp.zeros((pad_rows + TOKENS, HEADS_KV, HEAD_DIM), jnp.float32)
    (key_acc, value_acc), attended_all = lax.scan(block_step, (empty_acc, empty_acc), jnp.arange(N_CTX, dtype=jnp.int32))
    attention = attended_all.reshape(TOKENS, HEADS_Q * HEAD_DIM)
    key_grad = unrotate(key_acc[pad_rows:], cosine, sine_table).astype(jnp.bfloat16).reshape(TOKENS, HEADS_KV * HEAD_DIM)
    value_grad = value_acc[pad_rows:].astype(jnp.bfloat16).reshape(TOKENS, HEADS_KV * HEAD_DIM)
    pair_grads = jnp.concatenate([key_grad, value_grad], axis=1)

    def token_step(running, block_index):
        first_row = (block_index * TOK_DEV).astype(jnp.int32)
        feature_rows = lax.dynamic_slice_in_dim(features, first_row, TOK_DEV, 0)
        grad_rows = lax.dynamic_slice_in_dim(pair_grads, first_row, TOK_DEV, 0)
        term = jnp.dot(feature_rows.T, grad_rows, preferred_element_type=jnp.float32)
        return running + rounded(term), None

    weight_sum, unused_blocks = lax.scan(token_step, jnp.zeros((D, 2 * HEADS_KV * HEAD_DIM), jnp.float32), jnp.arange(N_CTX, dtype=jnp.int32))
    kv_width = HEADS_KV * HEAD_DIM
    return (attention, weight_sum[:, :kv_width].astype(jnp.bfloat16), weight_sum[:, kv_width:].astype(jnp.bfloat16))
```

```python
import jax
import jax.numpy as jnp
from jax import lax
from jax.sharding import Mesh, PartitionSpec as P

D = 5376
HEADS_Q = 32
HEAD_DIM = 128
WINDOW = 1024
SPAN = 2
CHUNKS = 4
CTX = ("chip", "core")


ROPE_BASE = 10000.0


def moved(block, distance):
    devices = range(lax.axis_size(CTX))
    route = [(i - distance, i) for i in devices if i - distance in devices]
    return lax.ppermute(block, CTX, route)


def from_partner(block, axis):
    return lax.ppermute(block, axis, [(0, 1), (1, 0)])


def rotate_half(values):
    middle = values.shape[-1] // 2
    return jnp.concatenate([-values[..., middle:], values[..., :middle]], axis=-1)


def rope_tables(offsets):
    middle = HEAD_DIM // 2
    inverse = ROPE_BASE ** (-(jnp.arange(middle).astype(jnp.float32) * 2.0 / HEAD_DIM))
    angles = offsets.astype(jnp.float32)[:, None] * inverse[None, :]
    cosine = jnp.cos(angles)
    sine_table = jnp.sin(angles)
    return (
        jnp.concatenate([cosine, cosine], axis=-1),
        jnp.concatenate([sine_table, sine_table], axis=-1),
    )


def rotate(values, cosine, sine_table):
    return values * cosine[:, None, :] + rotate_half(values) * sine_table[:, None, :]


def unrotate(values, cosine, sine_table):
    return values * cosine[:, None, :] - rotate_half(values) * sine_table[:, None, :]


def start_of(positions, starts):
    candidates = jnp.where(starts[None, :] <= positions[:, None], starts[None, :], -1)
    return jnp.max(candidates, axis=1)


def gather_features(features):
    if lax.axis_size("head") != 2:
        return lax.all_gather(features, "head", axis=1, tiled=True)
    mine = lax.axis_index("head") * features.shape[1]
    whole = jnp.zeros((features.shape[0], 2 * features.shape[1]), features.dtype)
    whole = lax.dynamic_update_slice(whole, features, (0, mine))
    return lax.dynamic_update_slice(
        whole, from_partner(features, "head"), (0, features.shape[1] - mine)
    )


def attend(grouped, key_block, value_block, grad_heads, allowed):
    scores = jnp.einsum("tkgd,skd->kgts", grouped, key_block, preferred_element_type=jnp.float32)
    row_max = jnp.max(jnp.where(allowed, scores, -jnp.inf), axis=-1, keepdims=True)
    raw_weights = jnp.where(allowed, jnp.exp(scores - row_max), 0.0)
    prob_soft = raw_weights / jnp.sum(raw_weights, axis=-1, keepdims=True)
    probs_low = prob_soft.astype(jnp.bfloat16)
    attended = jnp.einsum(
        "kgts,skd->tkgd", probs_low, value_block, preferred_element_type=jnp.float32
    ).astype(jnp.bfloat16)
    out_dot = jnp.sum(
        grad_heads.astype(jnp.float32) * attended.astype(jnp.float32), axis=-1
    ).transpose(1, 2, 0)[..., None]
    value_partial = jnp.einsum(
        "kgts,tkgd->skd", probs_low, grad_heads, preferred_element_type=jnp.float32
    )
    prob_grad = jnp.einsum(
        "tkgd,skd->kgts", grad_heads, value_block, preferred_element_type=jnp.float32
    )
    score_grad = (prob_soft * (prob_grad - out_dot)).astype(jnp.bfloat16)
    key_partial = jnp.einsum(
        "kgts,tkgd->skd", score_grad, grouped, preferred_element_type=jnp.float32
    )
    return attended, key_partial, value_partial


def shards(features, query_weight, key_weight, value_weight, doc_lengths, out_grad):
    tok_rows = features.shape[0]
    query_cols = query_weight.shape[1]
    value_cols = key_weight.shape[1]
    query_heads = query_cols // HEAD_DIM
    value_heads = value_cols // HEAD_DIM
    group_size = query_heads // value_heads
    query_scale = (D / HEADS_Q) ** (-0.5)
    chunks = min(CHUNKS, value_heads)
    chunk_heads = value_heads // chunks
    chunk_cols = value_cols // chunks
    ctx_index = lax.axis_index(CTX)
    core = lax.axis_index("core")

    def gathered_rows(piece):
        mine = lax.all_gather(piece, "chip", axis=0, tiled=True)
        return mine, from_partner(mine, "core")

    def projected(rows):
        mine, other = rows
        return jnp.dot(kept, mine, preferred_element_type=jnp.float32) + jnp.dot(
            given, other, preferred_element_type=jnp.float32
        )

    pair = min(2, chunks)
    kv_weights, q_weights = [], []
    for first in range(0, chunks, pair):
        cols = slice(first * chunk_cols, (first + pair) * chunk_cols)
        kv_weights.append(
            gathered_rows(jnp.concatenate([key_weight[:, cols], value_weight[:, cols]], axis=1))
        )
        for chunk in range(first, first + pair):
            width = chunk_cols * group_size
            q_weights.append(gathered_rows(query_weight[:, chunk * width : (chunk + 1) * width]))

    gathered = gather_features(features)
    chips = lax.axis_size("chip")
    by_core = gathered.reshape(tok_rows, chips, 2, D // (2 * chips))
    kept = lax.dynamic_index_in_dim(by_core, core, 2, keepdims=False).reshape(tok_rows, D // 2)
    given = lax.dynamic_index_in_dim(by_core, 1 - core, 2, keepdims=False).reshape(tok_rows, D // 2)
    chip_features = jnp.concatenate([kept, from_partner(given, "core")], axis=0)

    starts = jnp.cumsum(doc_lengths) - doc_lengths
    query_index = ctx_index * tok_rows + jnp.arange(tok_rows, dtype=jnp.int32)
    query_start = start_of(query_index, starts)
    cosine, sine_table = rope_tables(query_index - query_start)
    key_rows = (SPAN + 1) * tok_rows
    key_index = (ctx_index - SPAN) * tok_rows + jnp.arange(key_rows, dtype=jnp.int32)
    key_start = start_of(key_index, starts)
    offsets_qk = query_index[:, None] - key_index[None, :]
    allowed = (
        (key_index[None, :] >= 0)
        & (offsets_qk >= 0)
        & (offsets_qk < WINDOW)
        & (query_start[:, None] == key_start[None, :])
    )

    blocks = []
    for weights in kv_weights:
        proj = projected(weights)
        half = proj.shape[1] // 2
        own_keys = rotate(proj[:, :half].reshape(tok_rows, -1, HEAD_DIM), cosine, sine_table)
        own_values = proj[:, half:].reshape(tok_rows, -1, HEAD_DIM)
        key_value = jnp.stack([own_keys, own_values]).astype(jnp.bfloat16)
        earlier = []
        moving = key_value
        for distance in range(1, SPAN + 1):
            moving = moved(moving, 1)
            earlier.insert(0, moving)
        blocks.append(jnp.concatenate(earlier + [key_value], axis=1))

    attended, key_sums, value_sums = [], [], []
    for chunk in range(chunks):
        width = chunk_cols * group_size
        proj = projected(q_weights[chunk])
        grouped = (
            (rotate(proj.reshape(tok_rows, -1, HEAD_DIM), cosine, sine_table) * query_scale)
            .astype(jnp.bfloat16)
            .reshape(tok_rows, chunk_heads, group_size, HEAD_DIM)
        )
        at = chunk % pair
        block = blocks[chunk // pair][:, :, at * chunk_heads : (at + 1) * chunk_heads]
        grad_heads = out_grad[:, chunk * width : (chunk + 1) * width].reshape(
            tok_rows, chunk_heads, group_size, HEAD_DIM
        )
        out, key_partial, value_partial = attend(grouped, block[0], block[1], grad_heads, allowed)
        attended.append(out.reshape(tok_rows, width))
        partials = jnp.stack([key_partial, value_partial])

        def piece_of(distance):
            return partials[:, (SPAN - distance) * tok_rows : (SPAN - distance + 1) * tok_rows]

        returned = piece_of(SPAN)
        for distance in range(SPAN, 0, -1):
            returned = moved(returned.astype(jnp.bfloat16), -1).astype(jnp.float32) + piece_of(
                distance - 1
            )
        key_grad = unrotate(returned[0], cosine, sine_table).astype(jnp.bfloat16)
        value_grad = returned[1].astype(jnp.bfloat16)
        pair_grads = jnp.concatenate(
            [key_grad.reshape(tok_rows, chunk_cols), value_grad.reshape(tok_rows, chunk_cols)],
            axis=1,
        )
        chip_grads = jnp.concatenate([pair_grads, from_partner(pair_grads, "core")], axis=0)
        term = lax.dot_general(
            chip_features, chip_grads, (((0,), (0,)), ((), ())), preferred_element_type=jnp.float32
        ).astype(jnp.bfloat16)
        summed = lax.psum_scatter(term, "chip", scatter_dimension=0, tiled=True)
        key_sums.append(summed[:, :chunk_cols])
        value_sums.append(summed[:, chunk_cols:])
    return (
        jnp.concatenate(attended, axis=1),
        jnp.concatenate(key_sums, axis=1),
        jnp.concatenate(value_sums, axis=1),
    )


def solution(mesh):
    ctx, head = mesh.shape["ctx"], mesh.shape["head"]
    split = Mesh(mesh.devices.reshape(ctx // 2, 2, head), ("chip", "core", "head"))
    placed = P(CTX, "head")
    return jax.shard_map(
        shards,
        mesh=split,
        in_specs=(placed, placed, placed, placed, P(), placed),
        out_specs=(placed, placed, placed),
        check_vma=False,
    )
```

```python
import functools

import jax
import jax.numpy as jnp
from jax import lax
from jax.experimental import pallas as pl
from jax.experimental.pallas import tpu as pltpu
from jax.sharding import Mesh, PartitionSpec as P

D = 5376
HEADS_Q = 32
HEAD_DIM = 128
WINDOW = 1024
SPAN = 2
CTX = ("chip", "core")


ROPE_BASE = 10000.0


def moved(block, distance):
    devices = range(lax.axis_size(CTX))
    route = [(i - distance, i) for i in devices if i - distance in devices]
    return lax.ppermute(block, CTX, route)


def from_partner(block, axis):
    return lax.ppermute(block, axis, [(0, 1), (1, 0)])


def ring_of(chips):
    return list(range(0, chips, 2)) + list(range(chips - 1, 0, -2))


def along_ring(block, step):
    ring = ring_of(lax.axis_size("chip"))
    route = [(ring[i], ring[(i + step) % len(ring)]) for i in range(len(ring))]
    return lax.ppermute(block, "chip", route)


def ring_gather(shard):
    chips = lax.axis_size("chip")
    half = shard.shape[1] // 2
    found = {0: shard}
    ahead = behind = shard
    for step in range(1, chips // 2):
        behind, ahead = along_ring(behind, 1), along_ring(ahead, -1)
        found[step], found[chips - step] = ahead, behind
    found[chips // 2] = jnp.concatenate(
        [along_ring(behind[:, :half], 1), along_ring(ahead[:, half:], -1)], axis=1
    )
    return found


def ring_scatter(term):
    chips = lax.axis_size("chip")
    farthest = term(chips // 2).astype(jnp.bfloat16)
    half = farthest.shape[1] // 2
    onward, back = along_ring(farthest[:, :half], 1), along_ring(farthest[:, half:], -1)
    onward = jnp.pad(onward, ((0, 0), (0, half)))
    back = jnp.pad(back, ((0, 0), (half, 0)))
    for step in range(chips // 2 - 1, 0, -1):
        onward = along_ring((term(step) + onward.astype(jnp.float32)).astype(jnp.bfloat16), 1)
        back = along_ring((term(chips - step) + back.astype(jnp.float32)).astype(jnp.bfloat16), -1)
    return term(0) + onward.astype(jnp.float32) + back.astype(jnp.float32)


def rotate_half(values):
    middle = values.shape[-1] // 2
    return jnp.concatenate([-values[..., middle:], values[..., :middle]], axis=-1)


def rope_tables(offsets):
    middle = HEAD_DIM // 2
    inverse = ROPE_BASE ** (-(jnp.arange(middle).astype(jnp.float32) * 2.0 / HEAD_DIM))
    angles = offsets.astype(jnp.float32)[:, None] * inverse[None, :]
    cosine = jnp.cos(angles)
    sine_table = jnp.sin(angles)
    return (
        jnp.concatenate([cosine, cosine], axis=-1),
        jnp.concatenate([sine_table, sine_table], axis=-1),
    )


def rotate(values, cosine, sine_table):
    return values * cosine[:, None, :] + rotate_half(values) * sine_table[:, None, :]


def unrotate(values, cosine, sine_table):
    return values * cosine[:, None, :] - rotate_half(values) * sine_table[:, None, :]


def start_of(positions, starts):
    candidates = jnp.where(starts[None, :] <= positions[:, None], starts[None, :], -1)
    return jnp.max(candidates, axis=1)


def gather_features(features):
    if lax.axis_size("head") != 2:
        return lax.all_gather(features, "head", axis=1, tiled=True)
    mine = lax.axis_index("head") * features.shape[1]
    whole = jnp.zeros((features.shape[0], 2 * features.shape[1]), features.dtype)
    whole = lax.dynamic_update_slice(whole, features, (0, mine))
    return lax.dynamic_update_slice(
        whole, from_partner(features, "head"), (0, features.shape[1] - mine)
    )


QUERY_ROWS = 256


def attend_kernel(group_size, low_ref, q_ref, k_ref, v_ref, g_ref, out_ref, dk_ref, dv_ref):
    dk_ref[...] = jnp.zeros_like(dk_ref)
    dv_ref[...] = jnp.zeros_like(dv_ref)
    reach = WINDOW + QUERY_ROWS
    nt = (((1,), (1,)), ((), ()))
    tn = (((0,), (0,)), ((), ()))

    def mul(a, b, dims=(((1,), (0,)), ((), ()))):
        return lax.dot_general(a, b, dims, preferred_element_type=jnp.float32)

    for first in range(0, q_ref.shape[0], QUERY_ROWS):
        rows = slice(first, first + QUERY_ROWS)
        span = slice(first, first + reach)
        keys, values = k_ref[span, :], v_ref[span, :]
        key_at = lax.broadcasted_iota(jnp.int32, (reach, QUERY_ROWS), 0) + (first - WINDOW)
        query_at = lax.broadcasted_iota(jnp.int32, (reach, QUERY_ROWS), 1) + first
        allowed = (key_at >= low_ref[:, rows]) & (key_at <= query_at)
        for head in range(group_size):
            cols = slice(head * HEAD_DIM, (head + 1) * HEAD_DIM)
            query, grad = q_ref[rows, cols], g_ref[rows, cols]
            scores = jnp.where(allowed, mul(keys, query, nt), -jnp.inf)
            weights = jnp.exp(scores - jnp.max(scores, axis=0, keepdims=True))
            probs = weights * (1.0 / jnp.sum(weights, axis=0, keepdims=True))
            probs_low = probs.astype(jnp.bfloat16)
            attended = mul(values, probs_low, tn).astype(jnp.bfloat16).astype(jnp.float32)
            out_ref[rows, cols] = attended.T.astype(jnp.bfloat16)
            out_dot = jnp.sum(attended * grad.astype(jnp.float32).T, axis=0, keepdims=True)
            score_grad = (probs * (mul(values, grad, nt) - out_dot)).astype(jnp.bfloat16)
            dk_ref[span, :] += mul(score_grad, query)
            dv_ref[span, :] += mul(probs_low, grad)


def attend(low, queries, keys, values, grads):
    tok_rows, key_rows = queries.shape[0], keys.shape[0]
    heads = keys.shape[1] // HEAD_DIM
    group_size = queries.shape[1] // keys.shape[1]
    wide = pl.BlockSpec((tok_rows, group_size * HEAD_DIM), lambda h: (0, h))
    tall = pl.BlockSpec((key_rows, HEAD_DIM), lambda h: (0, h))
    sums = jax.ShapeDtypeStruct(keys.shape, jnp.float32)
    work = queries.shape[0] * queries.shape[1] * (WINDOW + QUERY_ROWS)
    return pl.pallas_call(
        functools.partial(attend_kernel, group_size),
        grid=(heads,),
        in_specs=[pl.BlockSpec((1, tok_rows), lambda h: (0, 0)), wide, tall, tall, wide],
        out_specs=[wide, tall, tall],
        out_shape=[jax.ShapeDtypeStruct(queries.shape, jnp.bfloat16), sums, sums],
        compiler_params=pltpu.CompilerParams(vmem_limit_bytes=40 * 1024 * 1024),
        cost_estimate=pl.CostEstimate(
            flops=10 * work, bytes_accessed=8 * queries.size + 12 * keys.size,
            transcendentals=work // HEAD_DIM,
        ),
    )(low, queries, keys, values, grads)


def shards(features, query_weight, key_weight, value_weight, doc_lengths, out_grad):
    tok_rows = features.shape[0]
    query_cols = query_weight.shape[1]
    value_cols = key_weight.shape[1]
    query_heads = query_cols // HEAD_DIM
    value_heads = value_cols // HEAD_DIM
    group_size = query_heads // value_heads
    query_scale = (D / HEADS_Q) ** (-0.5)
    ctx_index = lax.axis_index(CTX)
    core = lax.axis_index("core")

    gathered = gather_features(features)
    chips = lax.axis_size("chip")
    ring = ring_of(chips)
    place = jnp.asarray([ring.index(chip) for chip in range(chips)], jnp.int32)
    here = place[lax.axis_index("chip")]
    owners = jnp.asarray(ring, jnp.int32)[(here + jnp.arange(chips, dtype=jnp.int32)) % chips]
    by_owner = gathered.T.reshape(2 * chips, D // (2 * chips), tok_rows)

    def blocks_of(side):
        return jnp.concatenate(
            [
                lax.dynamic_index_in_dim(by_owner, owners[k] * 2 + side, 0, keepdims=False)
                for k in range(chips)
            ],
            axis=0,
        )

    kept, given = blocks_of(core), blocks_of(1 - core)
    chip_features = jnp.concatenate([kept, from_partner(given, "core")], axis=1)
    deep = D // (2 * chips)

    starts = jnp.cumsum(doc_lengths) - doc_lengths
    query_index = ctx_index * tok_rows + jnp.arange(tok_rows, dtype=jnp.int32)
    query_start = start_of(query_index, starts)
    cosine, sine_table = rope_tables(query_index - query_start)
    local = jnp.arange(tok_rows, dtype=jnp.int32)
    low = jnp.maximum(local - (WINDOW - 1), query_start - ctx_index * tok_rows)[None, :]

    def projected(shards_by_place):
        total = 0.0
        for k, mine in shards_by_place.items():
            rows = slice(k * deep, (k + 1) * deep)
            for block, weights in ((kept, mine), (given, from_partner(mine, "core"))):
                total = total + lax.dot_general(
                    block[rows], weights, (((0,), (0,)), ((), ())),
                    preferred_element_type=jnp.float32,
                )
        return total

    kv_shards = ring_gather(jnp.concatenate([key_weight, value_weight], axis=1))
    query_weight, early = lax.optimization_barrier((query_weight, kv_shards[2]))
    q_shards = ring_gather(query_weight)

    proj = projected(kv_shards)
    own_keys = rotate(proj[:, :value_cols].reshape(tok_rows, -1, HEAD_DIM), cosine, sine_table)
    own = jnp.concatenate([own_keys.reshape(tok_rows, value_cols), proj[:, value_cols:]], axis=1)
    own = own.astype(jnp.bfloat16)
    block = jnp.concatenate([moved(own, far) for far in range(SPAN, 0, -1)] + [own], axis=0)

    proj = projected(q_shards).reshape(tok_rows, query_heads, HEAD_DIM)
    queries = (rotate(proj, cosine, sine_table) * query_scale).astype(jnp.bfloat16)
    attended, key_partial, value_partial = attend(
        low,
        queries.reshape(tok_rows, query_cols),
        block[:, :value_cols],
        block[:, value_cols:],
        out_grad,
    )

    def returned(both):
        total = both[SPAN * tok_rows :]
        for far in range(1, SPAN + 1):
            piece = both[(SPAN - far) * tok_rows : (SPAN - far + 1) * tok_rows]
            total = total + moved(piece.astype(jnp.bfloat16), -far).astype(jnp.float32)
        return total

    key_grad = unrotate(
        returned(key_partial).reshape(tok_rows, value_heads, HEAD_DIM), cosine, sine_table
    ).reshape(tok_rows, value_cols)
    pair_grads = jnp.concatenate([key_grad, returned(value_partial)], axis=1).astype(jnp.bfloat16)
    chip_grads = jnp.concatenate([pair_grads, from_partner(pair_grads, "core")], axis=0)

    def term(k):
        return jnp.dot(
            chip_features[k * deep : (k + 1) * deep], chip_grads,
            preferred_element_type=jnp.float32,
        )

    weight_grads = ring_scatter(term)
    return (
        attended,
        weight_grads[:, :value_cols].astype(jnp.bfloat16),
        weight_grads[:, value_cols:].astype(jnp.bfloat16),
    )


def solution(mesh):
    ctx, head = mesh.shape["ctx"], mesh.shape["head"]
    split = Mesh(mesh.devices.reshape(ctx // 2, 2, head), ("chip", "core", "head"))
    placed = P(CTX, "head")
    return jax.shard_map(
        shards,
        mesh=split,
        in_specs=(placed, placed, placed, placed, P(), placed),
        out_specs=(placed, placed, placed),
        check_vma=False,
    )
```
